32 devices in a mesh: groups: 2 (over x), seq: 16 (over z, y, core).
Axes of the slice: x: 2, y: 2, z: 4, core: 2. Of those that a mesh axis runs over, the one named last changes fastest.
Arguments:
- queries: bfloat16 [24576, 2560], P(('groups', 'seq')), parts along dimension 0, may hold values from -30 to 30
- keys: bfloat16 [24576, 2560], P(('groups', 'seq')), parts along dimension 0, may hold values from -30 to 30
- values: bfloat16 [24576, 2560], P(('groups', 'seq')), parts along dimension 0, may hold values from -18 to 18
- lengths: int32 [16], P('groups'), parts along dimension 0, may hold values from 1 to 1536, as said below
- help_table: int32 [32, 2], P(('groups', 'seq')), parts along dimension 0, may hold values from -1 to 5, as said below
Outputs:
- attended: bfloat16 [24576, 2560], P(('groups', 'seq')), parts along dimension 0
- helped: bfloat16 [8192, 2560], P(('groups', 'seq')), parts along dimension 0
The draws below stay inside these ranges and needn't reach their ends.
There are 2 independent parts, one for each index of `groups`. The reference program is written for one: setup_inputs(seed, part) draws one part's arguments, and reference() takes and returns one part's arrays. A program takes and returns all parts, laid end to end along the dimension named above; each array names one. Nothing has to cross between parts.
Inputs may be any that keep to these rules, and one draw needn't show every extreme that they name: `lengths`: in each pair of candidates m, m + 4 one has more than 1408 valid tokens and the other at most 768; some candidate has exactly 1536 and some exactly 768. `help_table`: a device whose candidate is the shorter of its pair lists 2 distinct slab indices of its pair device; every other device has -1 in all slots.
All inputs are finite; a program needn't handle non-finite values.
Results may differ from the reference program's by a relative error of at most 0.0037.
Values may be sent and summed in bfloat16 or wider, within the bound.
No kernel may reach another device: no remote copies, remote signals or barrier semaphores. Data moves between devices by JAX's collectives and lax.ppermute only.
A program may use at most 128 MiB of HBM per device.

```python
import math
import jax
import jax.numpy as jnp
from jax import lax

HEADS = 20
HD = 128
ROWS = 768
SLAB = 128
HELP = 2
SPAN = 2
SLABS_DEV = 6
CAND = 8
CAP = 1536
TOKENS = 12288
N_SEQ = 16


def pair_layout(key):
    return jax.random.randint(jax.random.fold_in(key, 11), (CAND // 2,), 0, 2)


def draw_queries(key, part):
    shape = (TOKENS, HEADS * HD)
    key = jax.random.fold_in(key, 3)
    result = jnp.clip(1.4 * jax.random.normal(key, shape, jnp.float32), -8.4, 8.4)
    return result.astype(jnp.bfloat16)


def draw_keys(key, part):
    shape = (TOKENS, HEADS * HD)
    key = jax.random.fold_in(key, 4)
    result = jnp.clip(1.4 * jax.random.normal(key, shape, jnp.float32), -8.4, 8.4)
    return result.astype(jnp.bfloat16)


def draw_lengths(key, part):
    longer = pair_layout(key)
    key = jax.random.fold_in(key, 5)
    first_key, second_key = jax.random.split(key)
    long_len = CAP - jax.random.randint(first_key, (CAND // 2,), 0, SLAB)
    short_len = jax.random.randint(second_key, (CAND // 2,), 1, ROWS + 1)
    long_len = long_len.at[0].set(CAP)
    short_len = short_len.at[0].set(ROWS)
    first = jnp.where(longer == 0, long_len, short_len)
    second = jnp.where(longer == 0, short_len, long_len)
    return jnp.concatenate([first, second], axis=0).astype(jnp.int32)


def draw_help_table(key, part):
    longer = pair_layout(key)
    key = jax.random.fold_in(key, 6)
    devices = jnp.arange(N_SEQ)
    owner_cand = devices // SPAN
    place = devices % SPAN
    pair_index = owner_cand % (CAND // 2)
    half_index = owner_cand // (CAND // 2)
    is_short = half_index != longer[pair_index]
    offset = jax.random.randint(key, (N_SEQ,), 0, SLABS_DEV)
    offset = jnp.where(place == 0, 0, offset)
    slots = jnp.arange(HELP)
    chosen = jnp.mod(SLABS_DEV - 1 - slots[None, :] - offset[:, None], SLABS_DEV)
    return jnp.where(is_short[:, None], chosen, -1).astype(jnp.int32)


def steps_of(stream_key, dims, shards, least, high):
    loudness = 1.0
    for axis_at, parts in shards:
        draws = jax.random.uniform(jax.random.fold_in(jax.random.fold_in(stream_key, 6), axis_at), (parts,), jnp.float32, least / len(shards), high / len(shards))
        loudness = loudness * jnp.repeat(jnp.exp(draws), dims[axis_at] // parts).reshape((-1,) + (1,) * (len(dims) - 1 - axis_at))
    return loudness


def bell_draw(own_key, shape, spread, reach, cuts=(), kind=jnp.bfloat16):
    drawn = spread * jax.random.normal(own_key, shape, jnp.float32)
    if cuts:
        drawn = drawn * steps_of(own_key, shape, cuts, -0.22, 0.18)
    return jnp.clip(drawn, -reach, reach).astype(kind)


def setup_inputs(seed: int = 0, part: int = 0) -> dict:
    splits = jax.random.split(jax.random.key(seed), 6)
    part_keys = jax.random.split(jax.random.fold_in(splits[5], part), 6)
    queries = draw_queries(jax.random.fold_in(jax.random.fold_in(splits[5], part), 71), part)
    keys = draw_keys(jax.random.fold_in(jax.random.fold_in(splits[5], part), 71), part)
    values = bell_draw(part_keys[2], (TOKENS, HEADS * HD), 3.0, 18.0, ((0, 16),))
    lengths = draw_lengths(jax.random.fold_in(jax.random.fold_in(splits[5], part), 71), part)
    help_table = draw_help_table(jax.random.fold_in(jax.random.fold_in(splits[5], part), 71), part)
    return dict(queries=queries, keys=keys, values=values, lengths=lengths, help_table=help_table)


def attend_whole(query_block, key_block, value_block, length):
    query_wide = query_block.astype(jnp.float32).reshape(CAP, HEADS, HD)
    key_wide = key_block.astype(jnp.float32).reshape(CAP, HEADS, HD)
    value_wide = value_block.astype(jnp.float32).reshape(CAP, HEADS, HD)
    scores = jnp.einsum('rhd,khd->hrk', query_wide, key_wide) * (1.0 / math.sqrt(HD))
    valid_rows = jnp.arange(CAP) < length
    scores = jnp.where(valid_rows[None, None, :], scores, -jnp.inf)
    peak = lax.optimization_barrier(jnp.max(scores, axis=-1, keepdims=True))
    weights = jnp.exp(scores - peak)
    totals = lax.optimization_barrier(jnp.sum(weights, axis=-1))
    rounded = lax.optimization_barrier(weights.astype(jnp.bfloat16)).astype(jnp.float32)
    mixed = jnp.einsum('hrk,khd->rhd', rounded, value_wide) / jnp.transpose(totals)[:, :, None]
    mixed = jnp.where(valid_rows[:, None, None], mixed, 0.0)
    return mixed.reshape(CAP, HEADS * HD).astype(jnp.bfloat16)

def apply_attend(packed):
    return attend_whole(packed[0], packed[1], packed[2], packed[3])

def reference(queries, keys, values, lengths, help_table):
    feature_width = HEADS * HD
    home = lax.map(apply_attend, (queries.reshape(CAND, CAP, feature_width), keys.reshape(CAND, CAP, feature_width), values.reshape(CAND, CAP, feature_width), lengths))
    blocks = home.reshape(N_SEQ, SLABS_DEV, SLAB, feature_width)
    swapped_table = help_table.reshape(2, N_SEQ // 2, HELP)[::-1].reshape(N_SEQ, HELP)
    slab_ids = jnp.arange(SLABS_DEV).astype(jnp.int32)
    listed = jnp.any(swapped_table[:, None, :] == slab_ids[None, :, None], axis=-1)
    attended = jnp.where(listed[:, :, None, None], jnp.zeros((), jnp.bfloat16), blocks).reshape(TOKENS, feature_width)
    partner_blocks = blocks.reshape(2, N_SEQ // 2, SLABS_DEV, SLAB, feature_width)[::-1].reshape(N_SEQ, SLABS_DEV, SLAB, feature_width)
    selector = (help_table[:, :, None] == slab_ids[None, None, :]).astype(jnp.float32)
    helped = jnp.einsum('nhs,nstf->nhtf', selector, partner_blocks.astype(jnp.float32))
    helped = helped.astype(jnp.bfloat16).reshape(N_SEQ * HELP * SLAB, feature_width)
    return (attended, helped)
```

```python
import math

import jax
import jax.numpy as jnp
from jax import lax
from jax.experimental import pallas as pl
from jax.experimental.pallas import tpu as pltpu
from jax.sharding import PartitionSpec as P

HD = 128
SLAB = 128
SPAN = 2
KEY_TILE = 256
ROW_CHUNK = 16
STEP_HEADS = 2
WIDTH = STEP_HEADS * HD
SCALE = math.log2(math.e) / math.sqrt(HD)
CHUNK_HEADS = (4, 6, 10)


def rows_of(start):
    return pl.ds(pl.multiple_of(start, SLAB), SLAB)


def scaled_queries(ref, slabs, columns):
    wide = jnp.concatenate([ref[rows_of(s * SLAB), columns] for s in slabs], axis=0)
    wide = wide.astype(jnp.float32) * SCALE
    high = wide.astype(jnp.bfloat16)
    low = (wide - high.astype(jnp.float32)).astype(jnp.bfloat16)
    return jnp.concatenate([high, low], axis=1)


def key_tile(ref, start, columns, limit):
    tile = ref[pl.ds(start, KEY_TILE), columns]
    if limit is not None:
        first = ref[pl.ds(0, 16), columns].astype(jnp.float32)[0:1]
        valid = lax.broadcasted_iota(jnp.int32, tile.shape, 0) + start < limit
        tile = jnp.where(valid, tile.astype(jnp.float32), first).astype(jnp.bfloat16)
    return jnp.concatenate([tile, tile], axis=1)


def value_tile(ref, start, columns, limit):
    tile = ref[pl.ds(start, KEY_TILE), columns]
    ones = jnp.ones(tile.shape, jnp.bfloat16)
    if limit is not None:
        valid = lax.broadcasted_iota(jnp.int32, tile.shape, 0) + start < limit
        tile = jnp.where(valid, tile.astype(jnp.float32), 0.0).astype(jnp.bfloat16)
        ones = jnp.where(valid, 1.0, 0.0).astype(jnp.bfloat16)
    return jnp.concatenate([tile, ones], axis=1)


def attend(query_ref, pairs, mask_all, slab_sets, position, length, score_refs, weight_refs, store):
    tiles = []
    for key_ref, value_ref, limit in pairs:
        count = key_ref.shape[0] // KEY_TILE
        for t in range(count):
            masked = mask_all or t == count - 1
            tiles.append((key_ref, value_ref, t * KEY_TILE, limit if masked else None))
    total = len(tiles)
    keys = total * KEY_TILE
    items = [(h, slabs) for h in range(STEP_HEADS) for slabs in slab_sets]
    rows = SLAB * len(slab_sets[0])
    chunks = rows // ROW_CHUNK
    for t in range(len(items) + 2):
        now = items[t] if t < len(items) else None
        middle = 0 <= t - 1 < len(items)
        last = items[t - 2] if t >= 2 else None
        if now:
            now_columns = pl.ds(now[0] * HD, HD)
            scaled = scaled_queries(query_ref, now[1], now_columns)
        if last:
            last_columns = pl.ds(last[0] * HD, HD)
        mixed = None
        for j, (key_ref, value_ref, start, limit) in enumerate(tiles):
            if now:
                score_refs[t % 2][:rows, pl.ds(j * KEY_TILE, KEY_TILE)] = lax.dot_general(
                    scaled,
                    key_tile(key_ref, start, now_columns, limit),
                    (((1,), (1,)), ((), ())),
                    preferred_element_type=jnp.float32,
                )
            if last:
                part = jnp.dot(
                    weight_refs[t % 2][:rows, pl.ds(j * KEY_TILE, KEY_TILE)],
                    value_tile(value_ref, start, last_columns, limit),
                    preferred_element_type=jnp.float32,
                )
                mixed = part if mixed is None else mixed + part
            if middle:
                for c in range(j * chunks // total, (j + 1) * chunks // total):
                    here = pl.ds(c * ROW_CHUNK, ROW_CHUNK)
                    scores = score_refs[(t - 1) % 2][here, :keys]
                    peak = jnp.max(scores, axis=1, keepdims=True)
                    weight_refs[(t - 1) % 2][here, :keys] = jnp.exp2(scores - peak).astype(
                        jnp.bfloat16
                    )
        if last:
            result = mixed[:, :HD] / mixed[:, HD:]
            for n, slab in enumerate(last[1]):
                rows_at = position + slab * SLAB + lax.broadcasted_iota(jnp.int32, (SLAB, HD), 0)
                part = jnp.where(rows_at < length, result[n * SLAB : (n + 1) * SLAB], 0.0)
                store(last[0], n, slab, part.astype(jnp.bfloat16))


def limits(length, place, row_count):
    own = jnp.clip(length - place * row_count, 0, row_count)
    other = jnp.clip(length - (1 - place) * row_count, 0, row_count)
    return own, other


def help_body(me, lengths, listed, q, ko, vo, kx, vx, out, s0, s1, w0, w1):
    row_count = q.shape[0]
    length = lengths[me[0] // SPAN]
    place = me[0] % SPAN
    own, other = limits(length, place, row_count)
    active = listed[0, 0] >= 0

    @pl.when(active)
    def _():
        def store(h, n, slab, part):
            out[pl.ds(n * SLAB, SLAB), pl.ds(h * HD, HD)] = part

        attend(
            q, [(ko, vo, own), (kx, vx, other)], False, [[listed[0, 0], listed[0, 1]]],
            place * row_count, length, (s0, s1), (w0, w1), store,
        )

    @pl.when(jnp.logical_not(active))
    def _():
        out[...] = jnp.zeros_like(out)


def home_body(me, lengths, listed, q, ko, vo, kx, vx, *rest):
    out, s0, s1, w0, w1 = rest[-5:]
    row_count = q.shape[0]
    length = lengths[me[0] // SPAN]
    place = me[0] % SPAN
    own, other = limits(length, place, row_count)
    long = length > row_count
    low = jnp.minimum(listed[0, 0], listed[0, 1])
    high = jnp.maximum(listed[0, 0], listed[0, 1])

    def store(h, n, slab, part):
        out[rows_of(slab * SLAB), pl.ds(h * HD, HD)] = part

    @pl.when(long)
    def _():
        kept = []
        for n in range(row_count // SLAB - 2):
            slab = n + (n >= low).astype(jnp.int32)
            kept.append(slab + (slab >= high).astype(jnp.int32))
        half = len(kept) // 2
        attend(
            q, [(ko, vo, own), (kx, vx, other)], False, [kept[:half], kept[half:]],
            place * row_count, length, (s0, s1), (w0, w1), store,
        )
        for slab in (low, high):
            out[rows_of(slab * SLAB), :] = jnp.zeros((SLAB, WIDTH), jnp.bfloat16)

    @pl.when(jnp.logical_not(long) & (place == 0))
    def _():
        sets = [[n, n + 1] for n in range(0, row_count // SLAB, 2)]
        attend(q, [(ko, vo, own)], True, sets, 0, length, (s0, s1), (w0, w1), store)

    @pl.when(jnp.logical_not(long) & (place == 1))
    def _():
        out[...] = jnp.zeros_like(out)


def call(body, scalars, q, k, v, kx, vx, first, heads, rows, before=None):
    row_count, features = q.shape
    at = first // STEP_HEADS
    whole = pl.BlockSpec((row_count, WIDTH), lambda g, *_: (0, g + at))
    part = pl.BlockSpec((row_count, WIDTH), lambda g, *_: (0, g))
    in_specs = [whole, whole, whole, part, part]
    operands = [q, k, v, kx, vx]
    aliases = {}
    if rows == row_count:
        out_shape = jax.ShapeDtypeStruct((row_count, features), jnp.bfloat16)
        out_spec = whole
        if before is not None:
            in_specs.append(pl.BlockSpec(memory_space=pl.ANY))
            operands.append(before)
            aliases = {len(scalars) + 5: 0}
        worked = row_count - 2 * SLAB
    else:
        out_shape = jax.ShapeDtypeStruct((rows, heads * HD), jnp.bfloat16)
        out_spec = pl.BlockSpec((rows, WIDTH), lambda g, *_: (0, g))
        worked = rows
    item = 2 * SLAB
    scores = pltpu.VMEM((item, SPAN * row_count), jnp.float32)
    weights = pltpu.VMEM((item, SPAN * row_count), jnp.bfloat16)
    return pl.pallas_call(
        body,
        out_shape=out_shape,
        grid_spec=pltpu.PrefetchScalarGridSpec(
            num_scalar_prefetch=len(scalars),
            grid=(heads // STEP_HEADS,),
            in_specs=in_specs,
            out_specs=out_spec,
            scratch_shapes=[scores, scores, weights, weights],
        ),
        input_output_aliases=aliases,
        compiler_params=pltpu.CompilerParams(
            vmem_limit_bytes=40 << 20, dimension_semantics=("arbitrary",)
        ),
        cost_estimate=pl.CostEstimate(
            flops=8 * worked * SPAN * row_count * heads * HD,
            bytes_accessed=2 * 6 * row_count * heads * HD,
            transcendentals=worked * SPAN * row_count * heads,
        ),
    )(*scalars, *operands)


def local(queries, keys, values, lengths, help_table):
    row_count, features = queries.shape
    size = lax.axis_size("seq")
    core_pairs = [(i, i ^ 1) for i in range(size)]
    far_pairs = [(i, i ^ size // 2) for i in range(size)]
    listed = lax.ppermute(help_table, "seq", far_pairs)
    me = lax.axis_index("seq").astype(jnp.int32).reshape(1)
    scalars = (me, lengths, listed)

    edges = [0]
    for heads in CHUNK_HEADS:
        edges.append(edges[-1] + heads)
    assert edges[-1] * HD == features
    chunks = []
    for first, end in zip(edges[:-1], edges[1:]):
        part = (keys[:, first * HD : end * HD], values[:, first * HD : end * HD])
        chunks.append((first, end - first, lax.ppermute(part, "seq", core_pairs)))

    helped = []
    for first, heads, (kx, vx) in chunks:
        outputs = call(
            help_body, scalars, queries, keys, values, kx, vx, first, heads, help_table.shape[1] * SLAB
        )
        helped.append(lax.ppermute(outputs, "seq", far_pairs))
    attended = None
    for first, heads, (kx, vx) in chunks:
        attended = call(
            home_body, scalars, queries, keys, values, kx, vx, first, heads, row_count, attended
        )
    return attended, jnp.concatenate(helped, axis=1)


def solution(mesh):
    rows = P(("groups", "seq"), None)
    return jax.shard_map(
        local,
        mesh=mesh,
        in_specs=(rows, rows, rows, P("groups"), rows),
        out_specs=(rows, rows),
        check_vma=False,
    )
```

```python
import math

import jax
import jax.numpy as jnp
from jax import lax
from jax.experimental import pallas as pl
from jax.experimental.pallas import tpu as pltpu
from jax.sharding import PartitionSpec as P

HD = 128
SLAB = 128
SPAN = 2
KEY_TILE = 256
KEY_CHUNK = 32
STEP_HEADS = 2
WIDTH = STEP_HEADS * HD
SCALE = math.log2(math.e) / math.sqrt(HD)
EARLY_HEADS = (4,)
LATER_HEADS = (6, 10)


def rows_of(start):
    return pl.ds(pl.multiple_of(start, SLAB), SLAB)


def scaled_queries(ref, slabs, columns):
    wide = jnp.concatenate([ref[rows_of(s * SLAB), columns] for s in slabs], axis=0)
    wide = wide.astype(jnp.float32) * SCALE
    high = wide.astype(jnp.bfloat16)
    low = (wide - high.astype(jnp.float32)).astype(jnp.bfloat16)
    return jnp.concatenate([high, low], axis=1)


def attend(q, tiles, slabs, scratch, store, opening=False, closing=False):
    scores, weights, peaks, totals = scratch
    rows = SLAB * len(slabs)
    for t in range(STEP_HEADS):
        columns = pl.ds(t * HD, HD)
        before = (t - 1) % STEP_HEADS
        if not closing:
            scaled = scaled_queries(q, slabs, columns)
        if not opening:
            value_rows = [ref[pl.ds(start, KEY_TILE), columns] for _, ref, start, _ in tiles]
            mixed = lax.dot_general(
                jnp.concatenate(value_rows, axis=0),
                weights[t][...],
                (((0,), (0,)), ((), ())),
                preferred_element_type=jnp.float32,
            )
            mixed = mixed / totals[t][0:1, :]
        weigh = (t > 0 or not opening) and (t == 0 or not closing)
        peak = jnp.full((8, rows), -jnp.inf, jnp.float32)
        total = jnp.zeros((8, rows), jnp.float32)
        old_peak = peaks[(t - 1) % 2][0:1, :]
        for j, (key_ref, _, start, limit) in enumerate(tiles):
            if not closing:
                keys = key_ref[pl.ds(start, KEY_TILE), columns]
                made = lax.dot_general(
                    jnp.concatenate([keys, keys], axis=1),
                    scaled,
                    (((1,), (1,)), ((), ())),
                    preferred_element_type=jnp.float32,
                )
                if limit is not None:
                    valid = lax.broadcasted_iota(jnp.int32, made.shape, 0) + start < limit
                    made = jnp.where(valid, made, -jnp.inf)
                scores[t % 2][pl.ds(j * KEY_TILE, KEY_TILE), :] = made
                peak = jnp.maximum(peak, jnp.max(made.reshape(KEY_TILE // 8, 8, rows), axis=0))
            for c in range(0, KEY_TILE if weigh else 0, KEY_CHUNK):
                here = pl.ds(j * KEY_TILE + c, KEY_CHUNK)
                weight = jnp.exp2(scores[(t - 1) % 2][here, :] - old_peak)
                total = total + jnp.sum(weight.reshape(KEY_CHUNK // 8, 8, rows), axis=0)
                weights[before][here, :] = weight.astype(jnp.bfloat16)
        if not closing:
            peaks[t % 2][...] = jnp.broadcast_to(jnp.max(peak, axis=0, keepdims=True), peak.shape)
        if weigh:
            totals[before][...] = jnp.broadcast_to(
                jnp.sum(total, axis=0, keepdims=True), total.shape
            )
        if not opening:
            store(t, slabs, mixed.T)


def attend_steps(active, *operands):
    step, last = pl.program_id(0), pl.num_programs(0) - 1

    @pl.when(active & (step == 0))
    def _():
        attend(*operands, opening=True)

    @pl.when(active & (step > 0) & (step < last))
    def _():
        attend(*operands)

    @pl.when(active & (step == last))
    def _():
        attend(*operands, closing=True)


def long_tiles(ko, vo, kx, vx, length, place):
    row_count = ko.shape[0]
    tiles = []
    for key_ref, value_ref, at in ((ko, vo, place), (kx, vx, 1 - place)):
        limit = jnp.clip(length - at * row_count, 0, row_count)
        for start in range(0, row_count, KEY_TILE):
            last = start + KEY_TILE == row_count
            tiles.append((key_ref, value_ref, start, limit if last else None))
    return tiles


def valid_part(result, n, slab, place, row_count, length):
    at = place * row_count + slab * SLAB + lax.broadcasted_iota(jnp.int32, (SLAB, HD), 0)
    return jnp.where(at < length, result[n * SLAB : (n + 1) * SLAB], 0.0).astype(jnp.bfloat16)


def help_body(me, lengths, listed, q, ko, vo, kx, vx, out, *scratch):
    row_count = q.shape[0]
    length = lengths[me[0] // SPAN]
    place = me[0] % SPAN
    active = listed[0, 0] >= 0
    slabs = [jnp.maximum(listed[0, n], 0) for n in range(listed.shape[1])]

    def store(h, slabs, result):
        for n, slab in enumerate(slabs):
            part = valid_part(result, n, slab, place, row_count, length)
            out[pl.ds(n * SLAB, SLAB), pl.ds(h * HD, HD)] = part

    tiles = long_tiles(ko, vo, kx, vx, length, place)
    attend_steps(active, q, tiles, slabs, grouped(scratch), store)

    @pl.when(jnp.logical_not(active))
    def _():
        out[...] = jnp.zeros_like(out)


def home_body(me, lengths, listed, q, ko, vo, kx, vx, out, *scratch):
    row_count = q.shape[0]
    length = lengths[me[0] // SPAN]
    place = me[0] % SPAN
    long = length > row_count
    short = jnp.logical_not(long)
    low = jnp.clip(jnp.minimum(listed[0, 0], listed[0, 1]), 0, row_count // SLAB - 2)
    high = jnp.clip(jnp.maximum(listed[0, 0], listed[0, 1]), 1, row_count // SLAB - 1)

    def store(h, slabs, result):
        for n, slab in enumerate(slabs):
            part = valid_part(result, n, slab, place, row_count, length)
            out[rows_of(slab * SLAB), pl.ds(h * HD, HD)] = part

    kept = []
    for n in range(row_count // SLAB - 2):
        slab = n + (n >= low).astype(jnp.int32)
        kept.append(slab + (slab >= high).astype(jnp.int32))
    tiles = long_tiles(ko, vo, kx, vx, length, place)
    attend_steps(long, q, tiles, kept, grouped(scratch[: len(scratch) // 2]), store)

    @pl.when(long)
    def _():
        for slab in (low, high):
            out[rows_of(slab * SLAB), :] = jnp.zeros((SLAB, WIDTH), jnp.bfloat16)

    tiles = [(ko, vo, start, length) for start in range(0, row_count, KEY_TILE)]
    slabs = list(range(row_count // SLAB))
    attend_steps(
        short & (place == 0), q, tiles, slabs, grouped(scratch[len(scratch) // 2 :]), store
    )

    @pl.when(short & (place == 1))
    def _():
        out[...] = jnp.zeros_like(out)


def scratch_of(keys, rows):
    scores = [pltpu.VMEM((keys, rows), jnp.float32)] * 2
    weights = [pltpu.VMEM((keys, rows), jnp.bfloat16)] * STEP_HEADS
    sides = [pltpu.VMEM((8, rows), jnp.float32)] * (2 + STEP_HEADS)
    return scores + weights + sides


def grouped(refs):
    edges = (0, 2, 2 + STEP_HEADS, 4 + STEP_HEADS, 4 + 2 * STEP_HEADS)
    return [refs[a:b] for a, b in zip(edges[:-1], edges[1:])]


def call(body, scalars, q, k, v, kx, vx, first, heads, rows, k_first, v_first):
    row_count, features = q.shape
    steps = heads // STEP_HEADS

    def block(height, at, lag):
        if lag:
            return pl.BlockSpec((height, WIDTH), lambda g, *_: (0, at + jnp.maximum(g - 1, 0)))
        return pl.BlockSpec((height, WIDTH), lambda g, *_: (0, at + jnp.minimum(g, steps - 1)))

    at = first // STEP_HEADS
    home = rows == row_count
    item = rows - 2 * SLAB if home else rows
    scratch = scratch_of(SPAN * row_count, item)
    if home:
        scratch += scratch_of(row_count, row_count)
    return pl.pallas_call(
        body,
        out_shape=jax.ShapeDtypeStruct((rows, heads * HD), jnp.bfloat16),
        grid_spec=pltpu.PrefetchScalarGridSpec(
            num_scalar_prefetch=len(scalars),
            grid=(steps + 1,),
            in_specs=[
                block(row_count, at, 0),
                block(row_count, at, 0),
                block(row_count, at, 1),
                block(row_count, k_first // STEP_HEADS, 0),
                block(row_count, v_first // STEP_HEADS, 1),
            ],
            out_specs=block(rows, 0, 1),
            scratch_shapes=scratch,
        ),
        compiler_params=pltpu.CompilerParams(
            vmem_limit_bytes=60 << 20, dimension_semantics=("arbitrary",)
        ),
        cost_estimate=pl.CostEstimate(
            flops=8 * item * SPAN * row_count * heads * HD,
            bytes_accessed=2 * 6 * row_count * heads * HD,
            transcendentals=item * SPAN * row_count * heads,
        ),
    )(*scalars, q, k, v, kx, vx)


def local(queries, keys, values, lengths, help_table):
    row_count, features = queries.shape
    size = lax.axis_size("seq")
    core_pairs = [(i, i ^ 1) for i in range(size)]
    far_pairs = [(i, i ^ size // 2) for i in range(size)]
    me = lax.axis_index("seq").astype(jnp.int32).reshape(1)
    listed_rows = help_table.shape[1] * SLAB

    sources = []
    first = 0
    packed = []
    for heads in EARLY_HEADS:
        columns = slice(first * HD, (first + heads) * HD)
        packed += [keys[:, columns], values[:, columns]]
        first += heads
    packed = lax.ppermute(packed, "seq", core_pairs)
    listed = lax.ppermute(help_table, "seq", far_pairs)
    first = 0
    for n, heads in enumerate(EARLY_HEADS):
        sources.append((packed[2 * n], packed[2 * n + 1], first, heads, 0, 0))
        first += heads
    keys_whole, values_whole, listed, *_ = lax.optimization_barrier(
        (keys, values, listed, *packed)
    )
    kx, vx = lax.ppermute((keys_whole, values_whole), "seq", core_pairs)
    for heads in LATER_HEADS:
        sources.append((kx, vx, first, heads, first, first))
        first += heads
    assert first * HD == features

    scalars = (me, lengths, listed)
    helped = []
    for kx_n, vx_n, first, heads, k_first, v_first in sources:
        outputs = call(
            help_body, scalars, queries, keys, values, kx_n, vx_n, first, heads, listed_rows,
            k_first, v_first,
        )
        helped.append(lax.ppermute(outputs, "seq", far_pairs))
    attended = call(
        home_body, scalars, queries, keys, values, kx, vx, 0, features // HD, row_count, 0, 0
    )
    return attended, jnp.concatenate(helped, axis=1)


def solution(mesh):
    rows = P(("groups", "seq"), None)
    return jax.shard_map(
        local,
        mesh=mesh,
        in_specs=(rows, rows, rows, P("groups"), rows),
        out_specs=(rows, rows),
        check_vma=False,
    )
```

```python
import math

import jax
import jax.numpy as jnp
from jax import lax
from jax.experimental import pallas as pl
from jax.experimental.pallas import tpu as pltpu
from jax.sharding import PartitionSpec as P

HD = 128
SLAB = 128
SPAN = 2
KEY_TILE = 256
KEY_CHUNK = 32
STEP_HEADS = 2
WIDTH = STEP_HEADS * HD
SCALE = math.log2(math.e) / math.sqrt(HD)
EARLY_HEADS = (2, 4)
LATER_HEADS = (6, 8)
HELP_VMEM = 16 << 20
HOME_VMEM = 26 << 20


def rows_of(start):
    return pl.ds(pl.multiple_of(start, SLAB), SLAB)


def scaled_queries(ref, slabs, columns):
    wide = jnp.concatenate([ref[rows_of(s * SLAB), columns] for s in slabs], axis=0)
    wide = wide.astype(jnp.float32) * SCALE
    high = wide.astype(jnp.bfloat16)
    low = (wide - high.astype(jnp.float32)).astype(jnp.bfloat16)
    return jnp.concatenate([high, low], axis=1)


def attend(q, tiles, slabs, scratch, store, opening=False, closing=False):
    scores, weights, peaks, totals = scratch
    rows = SLAB * len(slabs)
    for t in range(STEP_HEADS):
        columns = pl.ds(t * HD, HD)
        before = (t - 1) % STEP_HEADS
        if not closing:
            scaled = scaled_queries(q, slabs, columns)
        if not opening:
            value_rows = [ref[pl.ds(start, KEY_TILE), columns] for _, ref, start, _ in tiles]
            mixed = lax.dot_general(
                jnp.concatenate(value_rows, axis=0),
                weights[t][...],
                (((0,), (0,)), ((), ())),
                preferred_element_type=jnp.float32,
            )
            mixed = mixed / totals[t][0:1, :]
        weigh = (t > 0 or not opening) and (t == 0 or not closing)
        peak = jnp.full((8, rows), -jnp.inf, jnp.float32)
        total = jnp.zeros((8, rows), jnp.float32)
        old_peak = peaks[(t - 1) % 2][0:1, :]
        for j, (key_ref, _, start, limit) in enumerate(tiles):
            if not closing:
                keys = key_ref[pl.ds(start, KEY_TILE), columns]
                made = lax.dot_general(
                    jnp.concatenate([keys, keys], axis=1),
                    scaled,
                    (((1,), (1,)), ((), ())),
                    preferred_element_type=jnp.float32,
                )
                if limit is not None:
                    valid = lax.broadcasted_iota(jnp.int32, made.shape, 0) + start < limit
                    made = jnp.where(valid, made, -jnp.inf)
                scores[t % 2][pl.ds(j * KEY_TILE, KEY_TILE), :] = made
                peak = jnp.maximum(peak, jnp.max(made.reshape(KEY_TILE // 8, 8, rows), axis=0))
            for c in range(0, KEY_TILE if weigh else 0, KEY_CHUNK):
                here = pl.ds(j * KEY_TILE + c, KEY_CHUNK)
                weight = jnp.exp2(scores[(t - 1) % 2][here, :] - old_peak)
                total = total + jnp.sum(weight.reshape(KEY_CHUNK // 8, 8, rows), axis=0)
                weights[before][here, :] = weight.astype(jnp.bfloat16)
        if not closing:
            peaks[t % 2][...] = jnp.broadcast_to(jnp.max(peak, axis=0, keepdims=True), peak.shape)
        if weigh:
            totals[before][...] = jnp.broadcast_to(
                jnp.sum(total, axis=0, keepdims=True), total.shape
            )
        if not opening:
            store(t, slabs, mixed.T)


def attend_steps(active, *operands):
    step, last = pl.program_id(0), pl.num_programs(0) - 1

    @pl.when(active & (step == 0))
    def _():
        attend(*operands, opening=True)

    @pl.when(active & (step > 0) & (step < last))
    def _():
        attend(*operands)

    @pl.when(active & (step == last))
    def _():
        attend(*operands, closing=True)


def long_tiles(ko, vo, kx, vx, length, place):
    row_count = ko.shape[0]
    tiles = []
    for key_ref, value_ref, at in ((ko, vo, place), (kx, vx, 1 - place)):
        limit = jnp.clip(length - at * row_count, 0, row_count)
        for start in range(0, row_count, KEY_TILE):
            last = start + KEY_TILE == row_count
            tiles.append((key_ref, value_ref, start, limit if last else None))
    return tiles


def valid_part(result, n, slab, place, row_count, length):
    at = place * row_count + slab * SLAB + lax.broadcasted_iota(jnp.int32, (SLAB, HD), 0)
    return jnp.where(at < length, result[n * SLAB : (n + 1) * SLAB], 0.0).astype(jnp.bfloat16)


def help_body(me, lengths, listed, q, ko, vo, kx, vx, out, *scratch):
    row_count = q.shape[0]
    length = lengths[me[0] // SPAN]
    place = me[0] % SPAN
    active = listed[0, 0] >= 0
    slabs = [jnp.maximum(listed[0, n], 0) for n in range(listed.shape[1])]

    def store(h, slabs, result):
        for n, slab in enumerate(slabs):
            part = valid_part(result, n, slab, place, row_count, length)
            out[pl.ds(n * SLAB, SLAB), pl.ds(h * HD, HD)] = part

    tiles = long_tiles(ko, vo, kx, vx, length, place)
    attend_steps(active, q, tiles, slabs, grouped(scratch), store)

    @pl.when(jnp.logical_not(active))
    def _():
        out[...] = jnp.zeros_like(out)


def home_body(me, lengths, listed, q, ko, vo, kx, vx, out, *scratch):
    row_count = q.shape[0]
    length = lengths[me[0] // SPAN]
    place = me[0] % SPAN
    long = length > row_count
    short = jnp.logical_not(long)
    low = jnp.clip(jnp.minimum(listed[0, 0], listed[0, 1]), 0, row_count // SLAB - 2)
    high = jnp.clip(jnp.maximum(listed[0, 0], listed[0, 1]), 1, row_count // SLAB - 1)

    def store(h, slabs, result):
        for n, slab in enumerate(slabs):
            part = valid_part(result, n, slab, place, row_count, length)
            out[rows_of(slab * SLAB), pl.ds(h * HD, HD)] = part

    kept = []
    for n in range(row_count // SLAB - 2):
        slab = n + (n >= low).astype(jnp.int32)
        kept.append(slab + (slab >= high).astype(jnp.int32))
    tiles = long_tiles(ko, vo, kx, vx, length, place)
    attend_steps(long, q, tiles, kept, grouped(scratch[: len(scratch) // 2]), store)

    @pl.when(long)
    def _():
        for slab in (low, high):
            out[rows_of(slab * SLAB), :] = jnp.zeros((SLAB, WIDTH), jnp.bfloat16)

    tiles = [(ko, vo, start, length) for start in range(0, row_count, KEY_TILE)]
    slabs = list(range(row_count // SLAB))
    attend_steps(
        short & (place == 0), q, tiles, slabs, grouped(scratch[len(scratch) // 2 :]), store
    )

    @pl.when(short & (place == 1))
    def _():
        out[...] = jnp.zeros_like(out)


def scratch_of(keys, rows):
    scores = [pltpu.VMEM((keys, rows), jnp.float32)] * 2
    weights = [pltpu.VMEM((keys, rows), jnp.bfloat16)] * STEP_HEADS
    sides = [pltpu.VMEM((8, rows), jnp.float32)] * (2 + STEP_HEADS)
    return scores + weights + sides


def grouped(refs):
    edges = (0, 2, 2 + STEP_HEADS, 4 + STEP_HEADS, 4 + 2 * STEP_HEADS)
    return [refs[a:b] for a, b in zip(edges[:-1], edges[1:])]


def call(body, scalars, arrays, first, heads, rows, vmem):
    row_count = arrays[0].shape[0]
    steps = heads // STEP_HEADS

    def block(height, at, lag):
        if lag:
            return pl.BlockSpec((height, WIDTH), lambda g, *_: (0, at + jnp.maximum(g - 1, 0)))
        return pl.BlockSpec((height, WIDTH), lambda g, *_: (0, at + jnp.minimum(g, steps - 1)))

    at = first // STEP_HEADS
    home = rows == row_count
    item = rows - 2 * SLAB if home else rows
    scratch = scratch_of(SPAN * row_count, item)
    if home:
        scratch += scratch_of(row_count, row_count)
    return pl.pallas_call(
        body,
        out_shape=jax.ShapeDtypeStruct((rows, heads * HD), jnp.bfloat16),
        grid_spec=pltpu.PrefetchScalarGridSpec(
            num_scalar_prefetch=len(scalars),
            grid=(steps + 1,),
            in_specs=[
                block(row_count, at, 0),
                block(row_count, at, 0),
                block(row_count, at, 1),
                block(row_count, at, 0),
                block(row_count, at, 1),
            ],
            out_specs=block(rows, 0, 1),
            scratch_shapes=scratch,
        ),
        compiler_params=pltpu.CompilerParams(
            vmem_limit_bytes=vmem, dimension_semantics=("arbitrary",)
        ),
        cost_estimate=pl.CostEstimate(
            flops=8 * item * SPAN * row_count * heads * HD,
            bytes_accessed=2 * 6 * row_count * heads * HD,
            transcendentals=item * SPAN * row_count * heads,
        ),
    )(*scalars, *arrays)


def local(queries, keys, values, lengths, help_table):
    row_count, features = queries.shape
    size = lax.axis_size("seq")
    core_pairs = [(i, i ^ 1) for i in range(size)]
    far_pairs = [(i, i ^ size // 2) for i in range(size)]
    me = lax.axis_index("seq").astype(jnp.int32).reshape(1)
    listed_rows = help_table.shape[1] * SLAB

    early = sum(EARLY_HEADS) * HD
    q_early, k_early, v_early = (x[:, :early] for x in (queries, keys, values))
    kx_early, vx_early = lax.ppermute((k_early, v_early), "seq", core_pairs)
    listed = lax.ppermute(help_table, "seq", far_pairs)
    keys_whole, values_whole, listed, _, _ = lax.optimization_barrier(
        (keys, values, listed, kx_early, vx_early)
    )
    kx, vx = lax.ppermute((keys_whole, values_whole), "seq", core_pairs)
    scalars = (me, lengths, listed)
    early_arrays = (q_early, k_early, v_early, kx_early, vx_early)
    arrays = (queries, keys, values, kx, vx)

    helped = []
    first = 0
    for n, heads in enumerate(EARLY_HEADS + LATER_HEADS):
        sources = early_arrays if n < len(EARLY_HEADS) else arrays
        outputs = call(help_body, scalars, sources, first, heads, listed_rows, HELP_VMEM)
        helped.append(lax.ppermute(outputs, "seq", far_pairs))
        first += heads
    assert first * HD == features
    attended = call(home_body, scalars, arrays, 0, first, row_count, HOME_VMEM)
    return attended, jnp.concatenate(helped, axis=1)


def solution(mesh):
    rows = P(("groups", "seq"), None)
    return jax.shard_map(
        local,
        mesh=mesh,
        in_specs=(rows, rows, rows, P("groups"), rows),
        out_specs=(rows, rows),
        check_vma=False,
    )
```

```python
import math

import jax
import jax.numpy as jnp
from jax import lax
from jax.experimental import pallas as pl
from jax.experimental.pallas import tpu as pltpu
from jax.sharding import PartitionSpec as P

HD = 128
SLAB = 128
SPAN = 2
KEY_TILE = 256
KEY_CHUNK = 32
STEP_HEADS = 2
WIDTH = STEP_HEADS * HD
SCALE = math.log2(math.e) / math.sqrt(HD)
EARLY_HEADS = (2, 4)
LATER_HEADS = (6, 8)
HELP_VMEM = 12 << 20
HOME_VMEM = 24 << 20


def rows_of(start):
    return pl.ds(pl.multiple_of(start, SLAB), SLAB)


def scaled_queries(ref, slabs, columns):
    wide = jnp.concatenate([ref[rows_of(s * SLAB), columns] for s in slabs], axis=0)
    wide = wide.astype(jnp.float32) * SCALE
    high = wide.astype(jnp.bfloat16)
    low = (wide - high.astype(jnp.float32)).astype(jnp.bfloat16)
    return jnp.concatenate([high, low], axis=1)


def attend(q, tiles, slabs, scratch, store, opening=False, closing=False):
    scores, weights, peaks, totals = scratch
    rows = SLAB * len(slabs)
    for t in range(STEP_HEADS):
        columns = pl.ds(t * HD, HD)
        before = (t - 1) % STEP_HEADS
        if not closing:
            scaled = scaled_queries(q, slabs, columns)
        if not opening:
            value_rows = [ref[pl.ds(start, KEY_TILE), columns] for _, ref, start, _ in tiles]
            mixed = lax.dot_general(
                jnp.concatenate(value_rows, axis=0),
                weights[t][...],
                (((0,), (0,)), ((), ())),
                preferred_element_type=jnp.float32,
            )
            mixed = mixed / totals[t][0:1, :]
        weigh = (t > 0 or not opening) and (t == 0 or not closing)
        peak = jnp.full((8, rows), -jnp.inf, jnp.float32)
        total = jnp.zeros((8, rows), jnp.float32)
        old_peak = peaks[(t - 1) % 2][0:1, :]
        for j, (key_ref, _, start, limit) in enumerate(tiles):
            if not closing:
                keys = key_ref[pl.ds(start, KEY_TILE), columns]
                made = lax.dot_general(
                    jnp.concatenate([keys, keys], axis=1),
                    scaled,
                    (((1,), (1,)), ((), ())),
                    preferred_element_type=jnp.float32,
                )
                if limit is not None:
                    valid = lax.broadcasted_iota(jnp.int32, made.shape, 0) + start < limit
                    made = jnp.where(valid, made, -jnp.inf)
                scores[t % 2][pl.ds(j * KEY_TILE, KEY_TILE), :] = made
                peak = jnp.maximum(peak, jnp.max(made.reshape(KEY_TILE // 8, 8, rows), axis=0))
            for c in range(0, KEY_TILE if weigh else 0, KEY_CHUNK):
                here = pl.ds(j * KEY_TILE + c, KEY_CHUNK)
                weight = jnp.exp2(scores[(t - 1) % 2][here, :] - old_peak)
                total = total + jnp.sum(weight.reshape(KEY_CHUNK // 8, 8, rows), axis=0)
                weights[before][here, :] = weight.astype(jnp.bfloat16)
        if not closing:
            peaks[t % 2][...] = jnp.broadcast_to(jnp.max(peak, axis=0, keepdims=True), peak.shape)
        if weigh:
            totals[before][...] = jnp.broadcast_to(
                jnp.sum(total, axis=0, keepdims=True), total.shape
            )
        if not opening:
            store(t, slabs, mixed.T)


def attend_steps(active, *operands):
    step, last = pl.program_id(0), pl.num_programs(0) - 1

    @pl.when(active & (step == 0))
    def _():
        attend(*operands, opening=True)

    @pl.when(active & (step > 0) & (step < last))
    def _():
        attend(*operands)

    @pl.when(active & (step == last))
    def _():
        attend(*operands, closing=True)


def long_tiles(ko, vo, kx, vx, length, place):
    row_count = ko.shape[0]
    tiles = []
    for key_ref, value_ref, at in ((ko, vo, place), (kx, vx, 1 - place)):
        limit = jnp.clip(length - at * row_count, 0, row_count)
        for start in range(0, row_count, KEY_TILE):
            last = start + KEY_TILE == row_count
            tiles.append((key_ref, value_ref, start, limit if last else None))
    return tiles


def valid_part(result, n, slab, place, row_count, length):
    at = place * row_count + slab * SLAB + lax.broadcasted_iota(jnp.int32, (SLAB, HD), 0)
    return jnp.where(at < length, result[n * SLAB : (n + 1) * SLAB], 0.0).astype(jnp.bfloat16)


def help_body(me, lengths, listed, q, ko, vo, kx, vx, out, *scratch):
    row_count = q.shape[0]
    length = lengths[me[0] // SPAN]
    place = me[0] % SPAN
    active = listed[0, 0] >= 0
    slabs = [jnp.maximum(listed[0, n], 0) for n in range(listed.shape[1])]

    def store(h, slabs, result):
        for n, slab in enumerate(slabs):
            part = valid_part(result, n, slab, place, row_count, length)
            out[pl.ds(n * SLAB, SLAB), pl.ds(h * HD, HD)] = part

    tiles = long_tiles(ko, vo, kx, vx, length, place)
    attend_steps(active, q, tiles, slabs, grouped(scratch), store)

    @pl.when(jnp.logical_not(active))
    def _():
        out[...] = jnp.zeros_like(out)


def home_body(me, lengths, listed, q, ko, vo, kx, vx, out, *scratch):
    row_count = q.shape[0]
    length = lengths[me[0] // SPAN]
    place = me[0] % SPAN
    long = length > row_count
    short = jnp.logical_not(long)
    low = jnp.clip(jnp.minimum(listed[0, 0], listed[0, 1]), 0, row_count // SLAB - 2)
    high = jnp.clip(jnp.maximum(listed[0, 0], listed[0, 1]), 1, row_count // SLAB - 1)

    def store(h, slabs, result):
        for n, slab in enumerate(slabs):
            part = valid_part(result, n, slab, place, row_count, length)
            out[rows_of(slab * SLAB), pl.ds(h * HD, HD)] = part

    kept = []
    for n in range(row_count // SLAB - 2):
        slab = n + (n >= low).astype(jnp.int32)
        kept.append(slab + (slab >= high).astype(jnp.int32))
    tiles = long_tiles(ko, vo, kx, vx, length, place)
    attend_steps(long, q, tiles, kept, grouped(scratch[: len(scratch) // 2]), store)

    @pl.when(long)
    def _():
        for slab in (low, high):
            out[rows_of(slab * SLAB), :] = jnp.zeros((SLAB, WIDTH), jnp.bfloat16)

    tiles = [(ko, vo, start, length) for start in range(0, row_count, KEY_TILE)]
    slabs = list(range(row_count // SLAB))
    attend_steps(
        short & (place == 0), q, tiles, slabs, grouped(scratch[len(scratch) // 2 :]), store
    )

    @pl.when(short & (place == 1))
    def _():
        out[...] = jnp.zeros_like(out)


def scratch_of(keys, rows):
    scores = [pltpu.VMEM((keys, rows), jnp.float32)] * 2
    weights = [pltpu.VMEM((keys, rows), jnp.bfloat16)] * STEP_HEADS
    sides = [pltpu.VMEM((8, rows), jnp.float32)] * (2 + STEP_HEADS)
    return scores + weights + sides


def grouped(refs):
    edges = (0, 2, 2 + STEP_HEADS, 4 + STEP_HEADS, 4 + 2 * STEP_HEADS)
    return [refs[a:b] for a, b in zip(edges[:-1], edges[1:])]


def call(body, scalars, arrays, first, heads, rows, vmem):
    row_count = arrays[0].shape[0]
    steps = heads // STEP_HEADS

    def block(height, at, lag):
        if lag:
            return pl.BlockSpec((height, WIDTH), lambda g, *_: (0, at + jnp.maximum(g - 1, 0)))
        return pl.BlockSpec((height, WIDTH), lambda g, *_: (0, at + jnp.minimum(g, steps - 1)))

    at = first // STEP_HEADS
    home = rows == row_count
    item = rows - 2 * SLAB if home else rows
    scratch = scratch_of(SPAN * row_count, item)
    if home:
        scratch += scratch_of(row_count, row_count)
    return pl.pallas_call(
        body,
        out_shape=jax.ShapeDtypeStruct((rows, heads * HD), jnp.bfloat16),
        grid_spec=pltpu.PrefetchScalarGridSpec(
            num_scalar_prefetch=len(scalars),
            grid=(steps + 1,),
            in_specs=[
                block(row_count, at, 0),
                block(row_count, at, 0),
                block(row_count, at, 1),
                block(row_count, at, 0),
                block(row_count, at, 1),
            ],
            out_specs=block(rows, 0, 1),
            scratch_shapes=scratch,
        ),
        compiler_params=pltpu.CompilerParams(
            vmem_limit_bytes=vmem, dimension_semantics=("arbitrary",)
        ),
        cost_estimate=pl.CostEstimate(
            flops=8 * item * SPAN * row_count * heads * HD,
            bytes_accessed=2 * 6 * row_count * heads * HD,
            transcendentals=item * SPAN * row_count * heads,
        ),
    )(*scalars, *arrays)


def local(queries, keys, values, lengths, help_table):
    row_count, features = queries.shape
    size = lax.axis_size("seq")
    core_pairs = [(i, i ^ 1) for i in range(size)]
    far_pairs = [(i, i ^ size // 2) for i in range(size)]
    me = lax.axis_index("seq").astype(jnp.int32).reshape(1)
    listed_rows = help_table.shape[1] * SLAB

    early = sum(EARLY_HEADS) * HD
    q_early, k_early, v_early = (x[:, :early] for x in (queries, keys, values))
    kx_early, vx_early = lax.ppermute((k_early, v_early), "seq", core_pairs)
    listed = lax.ppermute(help_table, "seq", far_pairs)
    keys_whole, values_whole, listed, kx_early, vx_early = lax.optimization_barrier(
        (keys, values, listed, kx_early, vx_early)
    )
    kx, vx = lax.ppermute((keys_whole, values_whole), "seq", core_pairs)
    scalars = (me, lengths, listed)
    early_arrays = (q_early, k_early, v_early, kx_early, vx_early)
    arrays = (queries, keys, values, kx, vx)

    helped = []
    first = 0
    for n, heads in enumerate(EARLY_HEADS + LATER_HEADS):
        sources = early_arrays if n < len(EARLY_HEADS) else arrays
        outputs = call(help_body, scalars, sources, first, heads, listed_rows, HELP_VMEM)
        helped.append(lax.ppermute(outputs, "seq", far_pairs))
        first += heads
    assert first * HD == features
    attended = call(home_body, scalars, arrays, 0, first, row_count, HOME_VMEM)
    return attended, jnp.concatenate(helped, axis=1)


def solution(mesh):
    rows = P(("groups", "seq"), None)
    return jax.shard_map(
        local,
        mesh=mesh,
        in_specs=(rows, rows, rows, P("groups"), rows),
        out_specs=(rows, rows),
        check_vma=False,
    )
```

```python
import math

import jax
import jax.numpy as jnp
from jax import lax
from jax.experimental import pallas as pl
from jax.experimental.pallas import tpu as pltpu
from jax.sharding import PartitionSpec as P

HD = 128
SLAB = 128
SPAN = 2
KEY_TILE = 256
KEY_CHUNK = 32
STEP_HEADS = 2
WIDTH = STEP_HEADS * HD
SCALE = math.log2(math.e) / math.sqrt(HD)
EARLY_HEADS = (2, 4)
LATER_HEADS = (8, 6)
HELP_VMEM = 16 << 20
HOME_VMEM = 26 << 20


def rows_of(start):
    return pl.ds(pl.multiple_of(start, SLAB), SLAB)


def scaled_queries(ref, slabs, columns):
    wide = jnp.concatenate([ref[rows_of(s * SLAB), columns] for s in slabs], axis=0)
    wide = wide.astype(jnp.float32) * SCALE
    high = wide.astype(jnp.bfloat16)
    low = (wide - high.astype(jnp.float32)).astype(jnp.bfloat16)
    return jnp.concatenate([high, low], axis=1)


def attend(q, tiles, slabs, scratch, store, opening=False, closing=False):
    scores, weights, peaks, totals = scratch
    rows = SLAB * len(slabs)
    for t in range(STEP_HEADS):
        columns = pl.ds(t * HD, HD)
        before = (t - 1) % STEP_HEADS
        if not closing:
            scaled = scaled_queries(q, slabs, columns)
        if not opening:
            value_rows = [ref[pl.ds(start, KEY_TILE), columns] for _, ref, start, _ in tiles]
            mixed = lax.dot_general(
                jnp.concatenate(value_rows, axis=0),
                weights[t][...],
                (((0,), (0,)), ((), ())),
                preferred_element_type=jnp.float32,
            )
            mixed = mixed / totals[t][0:1, :]
        weigh = (t > 0 or not opening) and (t == 0 or not closing)
        peak = jnp.full((8, rows), -jnp.inf, jnp.float32)
        total = jnp.zeros((8, rows), jnp.float32)
        old_peak = peaks[(t - 1) % 2][0:1, :]
        for j, (key_ref, _, start, limit) in enumerate(tiles):
            if not closing:
                keys = key_ref[pl.ds(start, KEY_TILE), columns]
                made = lax.dot_general(
                    jnp.concatenate([keys, keys], axis=1),
                    scaled,
                    (((1,), (1,)), ((), ())),
                    preferred_element_type=jnp.float32,
                )
                if limit is not None:
                    valid = lax.broadcasted_iota(jnp.int32, made.shape, 0) + start < limit
                    made = jnp.where(valid, made, -jnp.inf)
                scores[t % 2][pl.ds(j * KEY_TILE, KEY_TILE), :] = made
                peak = jnp.maximum(peak, jnp.max(made.reshape(KEY_TILE // 8, 8, rows), axis=0))
            for c in range(0, KEY_TILE if weigh else 0, KEY_CHUNK):
                here = pl.ds(j * KEY_TILE + c, KEY_CHUNK)
                weight = jnp.exp2(scores[(t - 1) % 2][here, :] - old_peak)
                total = total + jnp.sum(weight.reshape(KEY_CHUNK // 8, 8, rows), axis=0)
                weights[before][here, :] = weight.astype(jnp.bfloat16)
        if not closing:
            peaks[t % 2][...] = jnp.broadcast_to(jnp.max(peak, axis=0, keepdims=True), peak.shape)
        if weigh:
            totals[before][...] = jnp.broadcast_to(
                jnp.sum(total, axis=0, keepdims=True), total.shape
            )
        if not opening:
            store(t, slabs, mixed.T)


def attend_steps(active, *operands):
    step, last = pl.program_id(0), pl.num_programs(0) - 1

    @pl.when(active & (step == 0))
    def _():
        attend(*operands, opening=True)

    @pl.when(active & (step > 0) & (step < last))
    def _():
        attend(*operands)

    @pl.when(active & (step == last))
    def _():
        attend(*operands, closing=True)


def long_tiles(ko, vo, kx, vx, length, place):
    row_count = ko.shape[0]
    tiles = []
    for key_ref, value_ref, at in ((ko, vo, place), (kx, vx, 1 - place)):
        limit = jnp.clip(length - at * row_count, 0, row_count)
        for start in range(0, row_count, KEY_TILE):
            last = start + KEY_TILE == row_count
            tiles.append((key_ref, value_ref, start, limit if last else None))
    return tiles


def valid_part(result, n, slab, place, row_count, length):
    at = place * row_count + slab * SLAB + lax.broadcasted_iota(jnp.int32, (SLAB, HD), 0)
    return jnp.where(at < length, result[n * SLAB : (n + 1) * SLAB], 0.0).astype(jnp.bfloat16)


def help_body(me, lengths, listed, q, ko, vo, kx, vx, out, *scratch):
    row_count = q.shape[0]
    length = lengths[me[0] // SPAN]
    place = me[0] % SPAN
    active = listed[0, 0] >= 0
    slabs = [jnp.maximum(listed[0, n], 0) for n in range(listed.shape[1])]

    def store(h, slabs, result):
        for n, slab in enumerate(slabs):
            part = valid_part(result, n, slab, place, row_count, length)
            out[pl.ds(n * SLAB, SLAB), pl.ds(h * HD, HD)] = part

    tiles = long_tiles(ko, vo, kx, vx, length, place)
    attend_steps(active, q, tiles, slabs, grouped(scratch), store)

    @pl.when(jnp.logical_not(active))
    def _():
        out[...] = jnp.zeros_like(out)


def home_body(me, lengths, listed, q, ko, vo, kx, vx, out, *scratch):
    row_count = q.shape[0]
    length = lengths[me[0] // SPAN]
    place = me[0] % SPAN
    long = length > row_count
    short = jnp.logical_not(long)
    low = jnp.clip(jnp.minimum(listed[0, 0], listed[0, 1]), 0, row_count // SLAB - 2)
    high = jnp.clip(jnp.maximum(listed[0, 0], listed[0, 1]), 1, row_count // SLAB - 1)

    def store(h, slabs, result):
        for n, slab in enumerate(slabs):
            part = valid_part(result, n, slab, place, row_count, length)
            out[rows_of(slab * SLAB), pl.ds(h * HD, HD)] = part

    kept = []
    for n in range(row_count // SLAB - 2):
        slab = n + (n >= low).astype(jnp.int32)
        kept.append(slab + (slab >= high).astype(jnp.int32))
    tiles = long_tiles(ko, vo, kx, vx, length, place)
    attend_steps(long, q, tiles, kept, grouped(scratch[: len(scratch) // 2]), store)

    @pl.when(long)
    def _():
        for slab in (low, high):
            out[rows_of(slab * SLAB), :] = jnp.zeros((SLAB, WIDTH), jnp.bfloat16)

    tiles = [(ko, vo, start, length) for start in range(0, row_count, KEY_TILE)]
    slabs = list(range(row_count // SLAB))
    attend_steps(
        short & (place == 0), q, tiles, slabs, grouped(scratch[len(scratch) // 2 :]), store
    )

    @pl.when(short & (place == 1))
    def _():
        out[...] = jnp.zeros_like(out)


def scratch_of(keys, rows):
    scores = [pltpu.VMEM((keys, rows), jnp.float32)] * 2
    weights = [pltpu.VMEM((keys, rows), jnp.bfloat16)] * STEP_HEADS
    sides = [pltpu.VMEM((8, rows), jnp.float32)] * (2 + STEP_HEADS)
    return scores + weights + sides


def grouped(refs):
    edges = (0, 2, 2 + STEP_HEADS, 4 + STEP_HEADS, 4 + 2 * STEP_HEADS)
    return [refs[a:b] for a, b in zip(edges[:-1], edges[1:])]


def call(body, scalars, arrays, first, heads, rows, vmem):
    row_count = arrays[0].shape[0]
    steps = heads // STEP_HEADS

    def block(height, at, lag):
        if lag:
            return pl.BlockSpec((height, WIDTH), lambda g, *_: (0, at + jnp.maximum(g - 1, 0)))
        return pl.BlockSpec((height, WIDTH), lambda g, *_: (0, at + jnp.minimum(g, steps - 1)))

    at = first // STEP_HEADS
    home = rows == row_count
    item = rows - 2 * SLAB if home else rows
    scratch = scratch_of(SPAN * row_count, item)
    if home:
        scratch += scratch_of(row_count, row_count)
    return pl.pallas_call(
        body,
        out_shape=jax.ShapeDtypeStruct((rows, heads * HD), jnp.bfloat16),
        grid_spec=pltpu.PrefetchScalarGridSpec(
            num_scalar_prefetch=len(scalars),
            grid=(steps + 1,),
            in_specs=[
                block(row_count, at, 0),
                block(row_count, at, 0),
                block(row_count, at, 1),
                block(row_count, at, 0),
                block(row_count, at, 1),
            ],
            out_specs=block(rows, 0, 1),
            scratch_shapes=scratch,
        ),
        compiler_params=pltpu.CompilerParams(
            vmem_limit_bytes=vmem, dimension_semantics=("arbitrary",)
        ),
        cost_estimate=pl.CostEstimate(
            flops=8 * item * SPAN * row_count * heads * HD,
            bytes_accessed=2 * 6 * row_count * heads * HD,
            transcendentals=item * SPAN * row_count * heads,
        ),
    )(*scalars, *arrays)


def local(queries, keys, values, lengths, help_table):
    row_count, features = queries.shape
    size = lax.axis_size("seq")
    core_pairs = [(i, i ^ 1) for i in range(size)]
    far_pairs = [(i, i ^ size // 2) for i in range(size)]
    me = lax.axis_index("seq").astype(jnp.int32).reshape(1)
    listed_rows = help_table.shape[1] * SLAB

    early = sum(EARLY_HEADS) * HD
    q_early, k_early, v_early = (x[:, :early] for x in (queries, keys, values))
    kx_early, vx_early = lax.ppermute((k_early, v_early), "seq", core_pairs)
    listed = lax.ppermute(help_table, "seq", far_pairs)
    keys_whole, values_whole, listed, _, _ = lax.optimization_barrier(
        (keys, values, listed, kx_early, vx_early)
    )
    kx, vx = lax.ppermute((keys_whole, values_whole), "seq", core_pairs)
    scalars = (me, lengths, listed)
    early_arrays = (q_early, k_early, v_early, kx_early, vx_early)
    arrays = (queries, keys, values, kx, vx)

    helped = []
    first = 0
    for n, heads in enumerate(EARLY_HEADS + LATER_HEADS):
        sources = early_arrays if n < len(EARLY_HEADS) else arrays
        outputs = call(help_body, scalars, sources, first, heads, listed_rows, HELP_VMEM)
        helped.append(lax.ppermute(outputs, "seq", far_pairs))
        first += heads
    assert first * HD == features
    attended = call(home_body, scalars, arrays, 0, first, row_count, HOME_VMEM)
    return attended, jnp.concatenate(helped, axis=1)


def solution(mesh):
    rows = P(("groups", "seq"), None)
    return jax.shard_map(
        local,
        mesh=mesh,
        in_specs=(rows, rows, rows, P("groups"), rows),
        out_specs=(rows, rows),
        check_vma=False,
    )
```
